32 devices in a mesh: rep: 4 (over y, x), shard: 8 (over z, core).
Axes of the slice: x: 2, y: 2, z: 4, core: 2. Of those that a mesh axis runs over, the one named last changes fastest.
Arguments:
- images: bfloat16 [384, 14, 14, 512], P(('rep', 'shard')), may hold values from -6 to 6
- counts: int32 [32], P(('rep', 'shard')), may hold values from 3 to 12, as said below
- w_qkv: bfloat16 [512, 1536], P('shard'), may hold values from -0.25 to 0.25
- b_qv: bfloat16 [1024], P('shard'), may hold values from -3 to 3
- w_proj: bfloat16 [512, 512], P('shard'), may hold values from -0.75 to 0.75
- b_proj: bfloat16 [512], P('shard'), may hold values from -3 to 3
- w_fc1: bfloat16 [512, 2048], P('shard'), may hold values from -0.25 to 0.25
- b_fc1: bfloat16 [2048], P('shard'), may hold values from -3 to 3
- w_fc2: bfloat16 [2048, 512], P('shard'), may hold values from -0.1875 to 0.1875
- b_fc2: bfloat16 [512], P('shard'), may hold values from -3 to 3
- norm1_gain: bfloat16 [512], P('shard'), may hold values from 0.5 to 1.5
- norm1_shift: bfloat16 [512], P('shard'), may hold values from -2 to 2
- norm2_gain: bfloat16 [512], P('shard'), may hold values from 0.5 to 1.5
- norm2_shift: bfloat16 [512], P('shard'), may hold values from -2 to 2
- bias_table: bfloat16 [169, 16], replicated, may hold values from -3 to 3
- cotangent: bfloat16 [384, 14, 14, 512], P(('rep', 'shard')), may hold values from -6 to 6
Outputs:
- block_out: bfloat16 [384, 14, 14, 512], P(('rep', 'shard'))
- image_grad: float32 [384, 14, 14, 512], P(('rep', 'shard'))
- grad_w_qkv: float32 [512, 1536], P('shard')
- grad_b_qv: float32 [1024], P('shard')
- grad_w_proj: float32 [512, 512], P('shard')
- grad_b_proj: float32 [512], P('shard')
- grad_w_fc1: float32 [512, 2048], P('shard')
- grad_b_fc1: float32 [2048], P('shard')
- grad_w_fc2: float32 [2048, 512], P('shard')
- grad_b_fc2: float32 [512], P('shard')
- grad_norm1_gain: float32 [512], P('shard')
- grad_norm1_shift: float32 [512], P('shard')
- grad_norm2_gain: float32 [512], P('shard')
- grad_norm2_shift: float32 [512], P('shard')
- grad_bias_table: float32 [169, 16], replicated
The draws below stay inside these ranges and needn't reach their ends.
Inputs may be any that keep to these rules, and one draw needn't show every extreme that they name: counts[j] is the number of live image slots of device j: slots j * 12 to j * 12 + counts[j] - 1 hold images, the others are empty and give zero output and no gradient; some device holds 12.
All inputs are finite; a program needn't handle non-finite values.
Results may differ from the reference program's by a relative error of at most 0.018.
Values may be sent and summed in bfloat16 or wider, within the bound.
A program may use at most 128 MiB of HBM per device.

```python
import jax
import jax.numpy as jnp
from jax import lax

D = 512
HEADS = 16
MLP = 2048
SIDE = 14
WIN = 7
SHIFT = 3
TABLE = 169
IMG_CAP = 12
IMAGES = 384


def draw_counts(key, part):
    total_slots = IMAGES // IMG_CAP
    low_count = max(1, IMG_CAP // 4)
    key_counts = jax.random.fold_in(key, 11)
    key_pick = jax.random.fold_in(key, 23)
    drawn = jax.random.randint(key_counts, (total_slots,), low_count, IMG_CAP + 1, dtype=jnp.int32)
    chosen = jax.random.randint(key_pick, (), 0, total_slots, dtype=jnp.int32)
    return jnp.where(jnp.arange(total_slots, dtype=jnp.int32) == chosen, IMG_CAP, drawn).astype(jnp.int32)


def levels(rng, shape, pieces, smallest, top_value):
    level = 1.0
    for position, parts in pieces:
        heights = jax.random.uniform(jax.random.fold_in(jax.random.fold_in(rng, 6), position), (parts,), jnp.float32, smallest / len(pieces), top_value / len(pieces))
        level = level * jnp.repeat(jnp.exp(heights), shape[position] // parts).reshape((-1,) + (1,) * (len(shape) - 1 - position))
    return level


def scatter_about(key, extent, width, most, split=(), held_as=jnp.bfloat16):
    level = levels(key, extent, split, -0.22, 0.18) if split else 1.0
    values = jax.random.normal(key, extent, jnp.float32) * width * level
    return jnp.minimum(jnp.maximum(values, -most), most).astype(held_as)


def setup_inputs(seed: int = 0) -> dict:
    splits = jax.random.split(jax.random.key(seed), 17)
    return {
        "images": scatter_about(splits[0], (IMAGES, SIDE, SIDE, D), 1.0, 6.0, ((0, 32),)),
        "counts": draw_counts(jax.random.fold_in(splits[16], 71), 0),
        "w_qkv": scatter_about(splits[2], (D, 3 * D), D ** -0.5, 0.25, ((0, 8),)),
        "b_qv": scatter_about(splits[3], (2 * D,), 0.5, 3.0, ((0, 8),)),
        "w_proj": scatter_about(splits[4], (D, D), (D // 8) ** -0.5, 0.75, ((0, 8),)),
        "b_proj": scatter_about(splits[5], (D,), 0.5, 3.0, ((0, 8),)),
        "w_fc1": scatter_about(splits[6], (D, MLP), D ** -0.5, 0.25, ((0, 8),)),
        "b_fc1": scatter_about(splits[7], (MLP,), 0.5, 3.0, ((0, 8),)),
        "w_fc2": scatter_about(splits[8], (MLP, D), (MLP // 2) ** -0.5, 0.1875, ((0, 8),)),
        "b_fc2": scatter_about(splits[9], (D,), 0.5, 3.0, ((0, 8),)),
        "norm1_gain": jnp.clip(1.0 + 0.1 * jax.random.normal(splits[10], (D,), jnp.float32), 0.5, 1.5).astype(jnp.bfloat16),
        "norm1_shift": scatter_about(splits[11], (D,), 0.3, 2.0, ((0, 8),)),
        "norm2_gain": jnp.clip(1.0 + 0.1 * jax.random.normal(splits[12], (D,), jnp.float32), 0.5, 1.5).astype(jnp.bfloat16),
        "norm2_shift": scatter_about(splits[13], (D,), 0.3, 2.0, ((0, 8),)),
        "bias_table": scatter_about(splits[14], (TABLE, HEADS), 1.0, 3.0),
        "cotangent": scatter_about(splits[15], (IMAGES, SIDE, SIDE, D), 1.0, 6.0, ((0, 32),)),
    }


@jax.custom_vjp
def low(v):
    return lax.optimization_barrier(v.astype(jnp.bfloat16)).astype(jnp.float32)

@jax.custom_vjp
def low_back(v):
    return v

def low_keep(v):
    return (low(v), None)

def low_pass(kept, grad):
    return (grad,)

def back_keep(v):
    return (v, None)

def back_low(kept, grad):
    return (low(grad),)
low.defvjp(low_keep, low_pass)
low_back.defvjp(back_keep, back_low)

def layer_norm(values, gain, shift):
    center = values - lax.optimization_barrier(jnp.mean(values, axis=-1, keepdims=True))
    scaled = center * lax.rsqrt(lax.optimization_barrier(jnp.mean(center * center, axis=-1, keepdims=True)) + 1e-05)
    return scaled * gain + shift

def geometry():
    tokens = jnp.arange(SIDE * SIDE, dtype=jnp.int32)
    row_pos = tokens // SIDE
    col_pos = tokens % SIDE
    window_id = row_pos // WIN * (SIDE // WIN) + col_pos // WIN
    row_region = (row_pos >= SIDE - WIN).astype(jnp.int32) + (row_pos >= SIDE - SHIFT).astype(jnp.int32)
    col_region = (col_pos >= SIDE - WIN).astype(jnp.int32) + (col_pos >= SIDE - SHIFT).astype(jnp.int32)
    region = row_region * 3 + col_region
    same_window = window_id[:, None] == window_id[None, :]
    same_region = region[:, None] == region[None, :]
    row_local = row_pos % WIN
    col_local = col_pos % WIN
    relative = (row_local[:, None] - row_local[None, :] + WIN - 1) * (2 * WIN - 1) + col_local[:, None] - col_local[None, :] + WIN - 1
    relative = jnp.where(same_window, relative, 0).astype(jnp.int32)
    penalty = jnp.where(same_window, jnp.where(same_region, 0.0, -100.0), -1000000000.0).astype(jnp.float32)
    return (relative, penalty)

def swin_block(images, params):
    w_qkv, b_qv, w_proj, b_proj, w_fc1, b_fc1, w_fc2, b_fc2, gain_one, shift_one, gain_two, shift_two, bias_table = params
    relative, penalty = geometry()
    image_count = images.shape[0]
    tokens = SIDE * SIDE
    head_dim = D // HEADS
    heads_shape = (image_count, tokens, HEADS, head_dim)
    highest = lax.Precision.HIGHEST
    rolled = jnp.roll(images, (-SHIFT, -SHIFT), axis=(1, 2)).reshape(image_count, tokens, D)
    hidden_one = low(layer_norm(rolled, gain_one, shift_one))
    project = jnp.einsum('ntd,de->nte', hidden_one, w_qkv, precision=highest)
    query_heads = low(low_back(project[..., :D] + b_qv[:D])).reshape(heads_shape)
    key_heads = low(low_back(project[..., D:2 * D])).reshape(heads_shape)
    value_heads = low(low_back(project[..., 2 * D:] + b_qv[D:])).reshape(heads_shape)
    bias_full = jnp.transpose(bias_table[relative], (2, 0, 1)) + penalty[None]
    scores = jnp.einsum('nqhe,nkhe->nhqk', query_heads, key_heads, precision=highest) * head_dim ** (-0.5) + bias_full[None]
    scores = low_back(scores)
    probs_low = low(jax.nn.softmax(scores, axis=-1))
    attended = jnp.einsum('nhqk,nkhe->nqhe', probs_low, value_heads, precision=highest).reshape(image_count, tokens, D)
    attended = low(low_back(attended))
    branch = low_back(jnp.einsum('ntd,de->nte', attended, w_proj, precision=highest) + b_proj)
    residual = rolled + branch
    hidden_two = low(layer_norm(residual, gain_two, shift_two))
    pre_act = low_back(jnp.einsum('ntd,dm->ntm', hidden_two, w_fc1, precision=highest) + b_fc1)
    activated = low(jax.nn.gelu(pre_act, approximate=False))
    output = residual + low_back(jnp.einsum('ntm,md->ntd', activated, w_fc2, precision=highest) + b_fc2)
    return jnp.roll(output.reshape(image_count, SIDE, SIDE, D), (SHIFT, SHIFT), axis=(1, 2))

def reference(images, counts, w_qkv, b_qv, w_proj, b_proj, w_fc1, b_fc1, w_fc2, b_fc2, norm1_gain, norm1_shift, norm2_gain, norm2_shift, bias_table, cotangent):
    params = tuple((weight_item.astype(jnp.float32) for weight_item in (w_qkv, b_qv, w_proj, b_proj, w_fc1, b_fc1, w_fc2, b_fc2, norm1_gain, norm1_shift, norm2_gain, norm2_shift, bias_table)))
    groups = images.shape[0] // IMG_CAP
    slot_index = jnp.arange(IMG_CAP, dtype=jnp.int32)
    live_slot = (slot_index[None, :] < counts[:, None]).astype(jnp.float32)
    stacked = images.astype(jnp.float32).reshape(groups, IMG_CAP, SIDE, SIDE, D)
    cot_stack = cotangent.astype(jnp.float32).reshape(groups, IMG_CAP, SIDE, SIDE, D) * live_slot[:, :, None, None, None]

    def device_step(totals, inputs):
        group_images, group_cot = inputs
        result, pullback = jax.vjp(swin_block, group_images, params)
        image_part, param_grads = pullback(group_cot)
        return (jax.tree.map(jnp.add, totals, param_grads), (result, image_part))
    initial = jax.tree.map(jnp.zeros_like, params)
    totals, (results, image_parts) = lax.scan(device_step, initial, (stacked, cot_stack))
    block_out = (results * live_slot[:, :, None, None, None]).astype(jnp.bfloat16).reshape(images.shape)
    image_grad = image_parts.reshape(images.shape)
    return (block_out, image_grad, totals[0], totals[1], totals[2], totals[3], totals[4], totals[5], totals[6], totals[7], totals[8], totals[9], totals[10], totals[11], totals[12])
```

```python
import numpy as np

import jax
import jax.numpy as jnp
from jax import lax
from jax.experimental import pallas as pl
from jax.experimental.pallas import tpu as pltpu
from jax.sharding import PartitionSpec as P

D = 512
HEADS = 16
MLP = 2048
SIDE = 14
WIN = 7
SHIFT = 3
TABLE = 169
ROWS = 256
SCALE = (D // HEADS) ** -0.5
BF = jnp.bfloat16
F32 = jnp.float32


def place_matrix():
    place = np.zeros((ROWS, SIDE * 16), np.float32)
    for win in range(4):
        for tok in range(WIN * WIN):
            row = ((win // 2) * WIN + tok // WIN + SHIFT) % SIDE
            col = ((win % 2) * WIN + tok % WIN + SHIFT) % SIDE
            place[win * 64 + tok, row * 16 + col] = 1.0
    return place


def head_mask():
    rows, lanes = np.arange(512)[:, None], np.arange(256)[None, :]
    return (rows // 64 == lanes // 32).astype(np.float32)


def rel_index():
    tok = np.arange(WIN * WIN)
    r, c = tok // WIN, tok % WIN
    rel = (r[None, :] - r[:, None] + 6) * 13 + (c[None, :] - c[:, None] + 6)
    full = np.full((64, 64), -1)
    full[:49, :49] = rel
    return full.reshape(-1)


def penalty_term():
    out = np.zeros((4, 1, 64, 1, 64), np.float32)
    tok = np.arange(WIN * WIN)
    for win in range(4):
        row = (win // 2) * WIN + tok // WIN
        col = (win % 2) * WIN + tok % WIN
        reg = ((row >= 7) * 1 + (row >= 11)) * 3 + (col >= 7) * 1 + (col >= 11)
        out[win, 0, :49, 0, :49] = np.where(reg[:, None] == reg[None, :], 0.0, -100.0)
        out[win, 0, 49:] = -1e30
    return out


def nn(a, b):
    return jnp.dot(a, b, preferred_element_type=F32)


def nt(a, b):
    return lax.dot_general(a, b, (((1,), (1,)), ((), ())), preferred_element_type=F32)


def tn(a, b):
    return lax.dot_general(a, b, (((0,), (0,)), ((), ())), preferred_element_type=F32)


def norm_parts(x):
    center = x - jnp.mean(x, axis=-1, keepdims=True)
    inv = lax.rsqrt(jnp.mean(center * center, axis=-1, keepdims=True) + 1e-05)
    return center * inv, inv


def spread(block, mask):
    return jnp.concatenate([block] * 8, axis=0) * mask


def fold(full, mask):
    total = full[0:64] * mask[0:64]
    for h in range(1, 8):
        total += full[64 * h : 64 * h + 64] * mask[64 * h : 64 * h + 64]
    return total


def colsum(x):
    return jnp.sum(x, axis=0, keepdims=True)


def front_kernel(
    cnt, img, cot, place, mask, bias, w, bq, bv, gain, shift, xw_o, cw_o, qkv_o, pt_o, att_o, scr
):
    step = pl.program_id(0)

    @pl.when(step == 0)
    def _():
        scr[...] = jnp.zeros_like(scr)

    for r in range(SIDE):
        scr[pl.ds(16 * r, SIDE), :] = img[0, r]
    xw = nn(place[...], scr[...])
    xw_o[...] = xw.astype(BF)
    live = (step < cnt[0]).astype(F32)
    for r in range(SIDE):
        scr[pl.ds(16 * r, SIDE), :] = cot[0, r]
    cw_o[...] = (nn(place[...], scr[...]) * live).astype(BF)
    xhat, _ = norm_parts(xw)
    hidden = (xhat * gain[...] + shift[...]).astype(BF)
    qkv_o[:, :D] = (nn(hidden, w[:, :D]) + bq[...]).astype(BF)
    qkv_o[:, D : 2 * D] = nn(hidden, w[:, D : 2 * D]).astype(BF)
    qkv_o[:, 2 * D :] = (nn(hidden, w[:, 2 * D :]) + bv[...]).astype(BF)
    mask_low = mask[...]
    for win in range(4):
        rows = slice(64 * win, 64 * win + 64)
        for g in range(2):
            lo = 256 * g
            qb = spread(qkv_o[rows, lo : lo + 256], mask_low)
            st = nt(qkv_o[rows, D + lo : D + lo + 256], qb) * SCALE + bias[win, g]
            e = jnp.exp(st - jnp.max(st, axis=0, keepdims=True))
            p = (e / jnp.sum(e, axis=0, keepdims=True)).astype(BF)
            pt_o[0, win, g] = p
            full = tn(p, qkv_o[rows, 2 * D + lo : 2 * D + lo + 256])
            att_o[rows, lo : lo + 256] = fold(full, mask_low.astype(F32)).astype(BF)


def mlp_kernel(
    cnt, xw, cw, att, unplace, wp, w1, w2, bp, b1, b2, gain, shift,
    out_o, gr_o, ga_o, dwp_o, dw1_o, dw2_o, gbp, gb1, gb2, gg, gs,
    awp, aw1, aw2,
):
    step = pl.program_id(0)

    @pl.when(step == 0)
    def _():
        for ref in (awp, aw1, aw2, gbp, gb1, gb2, gg, gs):
            ref[...] = jnp.zeros_like(ref)

    res = xw[...].astype(F32) + (nn(att[...], wp[...]) + bp[...])
    xhat, inv = norm_parts(res)
    hidden = (xhat * gain[...] + shift[...]).astype(BF)
    g_low = cw[...]
    ff = jnp.zeros_like(res)
    gh = jnp.zeros_like(res)
    for j in range(4):
        cols = slice(512 * j, 512 * j + 512)
        pre = nn(hidden, w1[:, cols]) + b1[:, cols]
        half = 0.5 * (1.0 + lax.erf(pre * 0.7071067811865476))
        act = (pre * half).astype(BF)
        ff += nn(act, w2[cols, :])
        slope = half + pre * jnp.exp(-0.5 * pre * pre) * 0.3989422804014327
        gp32 = nt(g_low, w2[cols, :]) * slope
        gp = gp32.astype(BF)
        aw2[:, cols] += tn(g_low, act)
        aw1[:, cols] += tn(hidden, gp)
        gb1[:, cols] += colsum(gp.astype(F32))
        gh += nt(gp, w1[:, cols])
    out = res + (ff + b2[...])
    for i in range(2):
        live = (2 * step + i < cnt[0]).astype(F32)
        low = (out[ROWS * i : ROWS * i + ROWS] * live).astype(BF)
        back = nn(unplace[...], low).astype(BF)
        for r in range(SIDE):
            out_o[i, r] = back[16 * r : 16 * r + SIDE]
    g32 = g_low.astype(F32)
    gb2[...] += colsum(g32)
    gg[...] += colsum(gh * xhat)
    gs[...] += colsum(gh)
    e = gh * gain[...]
    gr = g32 + inv * (
        e - jnp.mean(e, axis=-1, keepdims=True) - xhat * jnp.mean(e * xhat, axis=-1, keepdims=True)
    )
    gr_o[...] = gr
    br = gr.astype(BF)
    gbp[...] += colsum(br.astype(F32))
    awp[...] += tn(att[...], br)
    ga_o[...] = nt(br, wp[...]).astype(BF)

    @pl.when(step == pl.num_programs(0) - 1)
    def _():
        dwp_o[...] = awp[...].astype(BF)
        dw1_o[...] = aw1[...].astype(BF)
        dw2_o[...] = aw2[...].astype(BF)


def back_kernel(
    xw, qkv, pt, ga, gr, unplace, mask, w, gain, shift,
    ig_o, dw_o, gbq, gbv, gg, gs, gbias, aw, gproj,
):
    step = pl.program_id(0)

    @pl.when(step == 0)
    def _():
        for ref in (aw, gbq, gbv, gg, gs, gbias):
            ref[...] = jnp.zeros_like(ref)

    mask_low = mask[...]
    for win in range(4):
        rows = slice(64 * win, 64 * win + 64)
        for g in range(2):
            lo = 256 * g
            db = spread(ga[rows, lo : lo + 256], mask_low)
            qb = spread(qkv[rows, lo : lo + 256], mask_low)
            p_low = pt[0, win, g]
            p = p_low.astype(F32)
            dp = nt(qkv[rows, 2 * D + lo : 2 * D + lo + 256], db)
            ds = (p * (dp - jnp.sum(p * dp, axis=0, keepdims=True))).astype(BF)
            gbias[g] += ds.astype(F32)
            gproj[rows, 2 * D + lo : 2 * D + lo + 256] = nn(p_low, db).astype(BF)
            gproj[rows, D + lo : D + lo + 256] = (nn(ds, qb) * SCALE).astype(BF)
            full = tn(ds, qkv[rows, D + lo : D + lo + 256])
            gproj[rows, lo : lo + 256] = (fold(full, mask_low.astype(F32)) * SCALE).astype(BF)
    gbq[...] += colsum(gproj[:, :D].astype(F32))
    gbv[...] += colsum(gproj[:, 2 * D :].astype(F32))
    xhat, inv = norm_parts(xw[...].astype(F32))
    hidden = (xhat * gain[...] + shift[...]).astype(BF)
    aw[...] += tn(hidden, gproj[...])
    gh = nt(gproj[...], w[...])
    gg[...] += colsum(gh * xhat)
    gs[...] += colsum(gh)
    e = gh * gain[...]
    grad = gr[...] + inv * (
        e - jnp.mean(e, axis=-1, keepdims=True) - xhat * jnp.mean(e * xhat, axis=-1, keepdims=True)
    )
    high = grad.astype(BF)
    low = (grad - high.astype(F32)).astype(BF)
    back = nn(unplace[...], high) + nn(unplace[...], low)
    for r in range(SIDE):
        ig_o[0, r] = back[16 * r : 16 * r + SIDE]

    @pl.when(step == pl.num_programs(0) - 1)
    def _():
        dw_o[...] = aw[...].astype(BF)


def whole(shape):
    return pl.BlockSpec(shape, lambda i: (0,) * len(shape))


def params():
    return pltpu.CompilerParams(
        dimension_semantics=("arbitrary",), vmem_limit_bytes=56 * 1024 * 1024
    )


def sds(shape, dtype):
    return jax.ShapeDtypeStruct(shape, dtype)


def body(
    images, counts, w_qkv, b_qv, w_proj, b_proj, w_fc1, b_fc1, w_fc2, b_fc2,
    norm1_gain, norm1_shift, norm2_gain, norm2_shift, bias_table, cotangent,
):
    n = images.shape[0]
    shards = lax.axis_size("shard")
    me = lax.axis_index("shard")
    vecs = (b_qv, b_proj, b_fc1, b_fc2, norm1_gain, norm1_shift, norm2_gain, norm2_shift)
    sizes = [v.shape[0] for v in vecs]
    packed = lax.all_gather(jnp.concatenate(vecs), "shard", axis=0).astype(F32)
    gw_qkv = lax.all_gather(w_qkv, "shard", axis=0, tiled=True)
    gw_proj = lax.all_gather(w_proj, "shard", axis=0, tiled=True)
    gw_fc1 = lax.all_gather(w_fc1, "shard", axis=0, tiled=True)
    gw_fc2 = lax.all_gather(w_fc2, "shard", axis=0, tiled=True)
    full, at = [], 0
    for size in sizes:
        full.append(packed[:, at : at + size].reshape(1, size * shards))
        at += size
    bqv, bp, b1, b2, g1, s1, g2, s2 = full

    place = place_matrix()
    place_in = jnp.asarray(place, BF)
    place_out = jnp.asarray(place.T, BF)
    mask = jnp.asarray(head_mask(), BF)
    rel = jnp.asarray(rel_index(), jnp.int32)
    onehot = (jnp.arange(TABLE, dtype=jnp.int32)[:, None] == rel[None, :]).astype(BF)
    bias = lax.dot_general(
        bias_table, onehot, (((0,), (0,)), ((), ())), preferred_element_type=F32
    ).reshape(2, 8, 64, 64).transpose(0, 2, 1, 3)
    bias = (bias[None] + jnp.asarray(penalty_term())).reshape(4, 2, 64, 512)

    smem = pl.BlockSpec(memory_space=pltpu.SMEM)
    image_spec = pl.BlockSpec((1, SIDE, SIDE, D), lambda i: (i, 0, 0, 0))
    rows = lambda count, width: pl.BlockSpec((count, width), lambda i: (i, 0))
    probs_spec = pl.BlockSpec((1, 4, 2, 64, 512), lambda i: (i, 0, 0, 0, 0))
    vec = whole((1, D))
    total = n * ROWS

    xw, cw, qkv, pt, att = pl.pallas_call(
        front_kernel,
        grid=(n,),
        in_specs=[
            smem, image_spec, image_spec, whole((ROWS, 224)), whole((512, 256)),
            whole((4, 2, 64, 512)), whole((D, 3 * D)), vec, vec, vec, vec,
        ],
        out_specs=[rows(ROWS, D), rows(ROWS, D), rows(ROWS, 3 * D), probs_spec, rows(ROWS, D)],
        out_shape=[
            sds((total, D), BF), sds((total, D), BF), sds((total, 3 * D), BF),
            sds((n, 4, 2, 64, 512), BF), sds((total, D), BF),
        ],
        scratch_shapes=[pltpu.VMEM((224, D), BF)],
        compiler_params=params(),
        cost_estimate=pl.CostEstimate(
            flops=60_000_000_000, bytes_accessed=30_000_000, transcendentals=0
        ),
        name="front",
    )(
        counts, images, cotangent, place_in, mask, bias, gw_qkv,
        bqv[:, :D], bqv[:, D:], g1, s1,
    )

    wide = whole((1, MLP))
    block_out, gr, ga, dwp, dw1, dw2t, gbp, gb1, gb2, gg2, gs2 = pl.pallas_call(
        mlp_kernel,
        grid=(n // 2,),
        in_specs=[
            smem, rows(512, D), rows(512, D), rows(512, D), whole((224, ROWS)),
            whole((D, D)), whole((D, MLP)), whole((MLP, D)), vec, wide, vec, vec, vec,
        ],
        out_specs=[
            pl.BlockSpec((2, SIDE, SIDE, D), lambda i: (i, 0, 0, 0)),
            rows(512, D), rows(512, D), whole((D, D)), whole((D, MLP)), whole((D, MLP)),
            vec, wide, vec, vec, vec,
        ],
        out_shape=[
            sds(images.shape, BF), sds((total, D), F32), sds((total, D), BF),
            sds((D, D), BF), sds((D, MLP), BF), sds((D, MLP), BF),
            sds((1, D), F32), sds((1, MLP), F32), sds((1, D), F32), sds((1, D), F32),
            sds((1, D), F32),
        ],
        scratch_shapes=[
            pltpu.VMEM((D, D), F32), pltpu.VMEM((D, MLP), F32), pltpu.VMEM((D, MLP), F32),
        ],
        compiler_params=params(),
        cost_estimate=pl.CostEstimate(
            flops=60_000_000_000, bytes_accessed=30_000_000, transcendentals=0
        ),
        name="mlp",
    )(counts, xw, cw, att, place_out, gw_proj, gw_fc1, gw_fc2, bp, b1, b2, g2, s2)

    def scatter(term):
        return lax.psum_scatter(term, "shard", scatter_dimension=0, tiled=True)

    own_mlp = (scatter(dwp), scatter(dw1), scatter(dw2t.T))

    image_grad, dwq, gbq, gbv, gg1, gs1, gbias = pl.pallas_call(
        back_kernel,
        grid=(n,),
        in_specs=[
            rows(ROWS, D), rows(ROWS, 3 * D), probs_spec, rows(ROWS, D), rows(ROWS, D),
            whole((224, ROWS)), whole((512, 256)), whole((D, 3 * D)), vec, vec,
        ],
        out_specs=[
            image_spec, whole((D, 3 * D)), vec, vec, vec, vec, whole((2, 64, 512)),
        ],
        out_shape=[
            sds(images.shape, F32), sds((D, 3 * D), BF), sds((1, D), F32), sds((1, D), F32),
            sds((1, D), F32), sds((1, D), F32), sds((2, 64, 512), F32),
        ],
        scratch_shapes=[pltpu.VMEM((D, 3 * D), F32), pltpu.VMEM((ROWS, 3 * D), BF)],
        compiler_params=params(),
        cost_estimate=pl.CostEstimate(
            flops=80_000_000_000, bytes_accessed=30_000_000, transcendentals=0
        ),
        name="back",
    )(xw, qkv, pt, ga, gr, place_out, mask, gw_qkv, g1, s1)

    own = (scatter(dwq),) + own_mlp
    own = [lax.psum(term, "rep").astype(F32) for term in own]
    by_head = gbias.reshape(2, 64, 8, 64).transpose(0, 2, 1, 3).reshape(HEADS, 4096)
    table = lax.dot_general(
        onehot.astype(F32), by_head, (((1,), (1,)), ((), ())),
        precision=lax.Precision.HIGHEST, preferred_element_type=F32,
    )
    terms = (jnp.concatenate([gbq, gbv], axis=1), gbp, gb1, gb2, gg1, gs1, gg2, gs2)
    flat = jnp.concatenate([t.reshape(-1) for t in terms] + [table.reshape(-1)])
    flat = lax.psum(flat, ("rep", "shard"))
    small, at = [], 0
    for size in sizes:
        small.append(lax.dynamic_slice_in_dim(flat, at + me * size, size))
        at += size * shards
    table = flat[at:].reshape(TABLE, HEADS)
    return (
        block_out, image_grad, own[0], small[0], own[1], small[1], own[2], small[2],
        own[3], small[3], small[4], small[5], small[6], small[7], table,
    )


def solution(mesh):
    img = P(("rep", "shard"), None, None, None)
    row, vec = P("shard", None), P("shard")
    weights = (row, vec, row, vec, row, vec, row, vec, vec, vec, vec, vec)
    return jax.shard_map(
        body,
        mesh=mesh,
        in_specs=(img, P(("rep", "shard"))) + weights + (P(), img),
        out_specs=(img, img) + weights + (P(),),
        check_vma=False,
    )
```

```python
import numpy as np

import jax
import jax.numpy as jnp
from jax import lax
from jax.experimental import pallas as pl
from jax.experimental.pallas import tpu as pltpu
from jax.sharding import PartitionSpec as P

D = 512
HEADS = 16
MLP = 2048
SIDE = 14
WIN = 7
SHIFT = 3
TABLE = 169
ROWS = 256
SCALE = (D // HEADS) ** -0.5
BF = jnp.bfloat16
F32 = jnp.float32


def place_matrix():
    place = np.zeros((ROWS, SIDE * 16), np.float32)
    for win in range(4):
        for tok in range(WIN * WIN):
            row = ((win // 2) * WIN + tok // WIN + SHIFT) % SIDE
            col = ((win % 2) * WIN + tok % WIN + SHIFT) % SIDE
            place[win * 64 + tok, row * 16 + col] = 1.0
    return place


def head_mask():
    rows, lanes = np.arange(512)[:, None], np.arange(256)[None, :]
    return (rows // 64 == lanes // 32).astype(np.float32)


def rel_index():
    tok = np.arange(WIN * WIN)
    r, c = tok // WIN, tok % WIN
    rel = (r[None, :] - r[:, None] + 6) * 13 + (c[None, :] - c[:, None] + 6)
    full = np.full((64, 64), -1)
    full[:49, :49] = rel
    return full.reshape(-1)


def penalty_term():
    out = np.zeros((4, 1, 64, 1, 64), np.float32)
    tok = np.arange(WIN * WIN)
    for win in range(4):
        row = (win // 2) * WIN + tok // WIN
        col = (win % 2) * WIN + tok % WIN
        reg = ((row >= 7) * 1 + (row >= 11)) * 3 + (col >= 7) * 1 + (col >= 11)
        out[win, 0, :49, 0, :49] = np.where(reg[:, None] == reg[None, :], 0.0, -100.0)
        out[win, 0, 49:] = -1e30
    return out


def nn(a, b):
    return jnp.dot(a, b, preferred_element_type=F32)


def nt(a, b):
    return lax.dot_general(a, b, (((1,), (1,)), ((), ())), preferred_element_type=F32)


def tn(a, b):
    return lax.dot_general(a, b, (((0,), (0,)), ((), ())), preferred_element_type=F32)


def norm_parts(x):
    center = x - jnp.mean(x, axis=-1, keepdims=True)
    inv = lax.rsqrt(jnp.mean(center * center, axis=-1, keepdims=True) + 1e-05)
    return center * inv, inv


def spread(block, mask):
    return jnp.concatenate([block] * 8, axis=0) * mask


def fold(full, mask):
    total = full[0:64] * mask[0:64]
    for h in range(1, 8):
        total += full[64 * h : 64 * h + 64] * mask[64 * h : 64 * h + 64]
    return total


def colsum(x):
    return jnp.sum(x, axis=0, keepdims=True)


def front_kernel(
    cnt, img, cot, place, mask, bias, w, bq, bv, gain, shift, xw_o, cw_o, qkv_o, pt_o, att_o, scr
):
    step = pl.program_id(0)

    @pl.when(step == 0)
    def _():
        scr[...] = jnp.zeros_like(scr)

    for r in range(SIDE):
        scr[pl.ds(16 * r, SIDE), :] = img[0, r]
    xw = nn(place[...], scr[...])
    xw_o[...] = xw.astype(BF)
    live = (step < cnt[0]).astype(F32)
    for r in range(SIDE):
        scr[pl.ds(16 * r, SIDE), :] = cot[0, r]
    cw_o[...] = (nn(place[...], scr[...]) * live).astype(BF)
    xhat, _ = norm_parts(xw)
    hidden = (xhat * gain[...] + shift[...]).astype(BF)
    qkv_o[:, :D] = (nn(hidden, w[:, :, :D].reshape(D, D)) + bq[...]).astype(BF)
    qkv_o[:, D : 2 * D] = nn(hidden, w[:, :, D : 2 * D].reshape(D, D)).astype(BF)
    qkv_o[:, 2 * D :] = (nn(hidden, w[:, :, 2 * D :].reshape(D, D)) + bv[...]).astype(BF)
    mask_low = mask[...]
    for win in range(4):
        rows = slice(64 * win, 64 * win + 64)
        for g in range(2):
            lo = 256 * g
            qb = spread(qkv_o[rows, lo : lo + 256], mask_low)
            st = nt(qkv_o[rows, D + lo : D + lo + 256], qb) * SCALE + bias[win, g]
            e = jnp.exp(st - jnp.max(st, axis=0, keepdims=True))
            p = (e / jnp.sum(e, axis=0, keepdims=True)).astype(BF)
            pt_o[0, win, g] = p
            full = tn(p, qkv_o[rows, 2 * D + lo : 2 * D + lo + 256])
            att_o[rows, lo : lo + 256] = fold(full, mask_low.astype(F32)).astype(BF)


def mlp_kernel(
    cnt, xw, cw, att, unplace, wp, w1, w2, bp, b1, b2, gain, shift,
    out_o, gr_o, ga_o, dwp_o, dw1_o, dw2_o, gbp, gb1, gb2, gg, gs,
    awp, aw1, aw2,
):
    step = pl.program_id(0)

    @pl.when(step == 0)
    def _():
        for ref in (awp, aw1, aw2, gbp, gb1, gb2, gg, gs):
            ref[...] = jnp.zeros_like(ref)

    res = xw[...].astype(F32) + (nn(att[...], wp[...]) + bp[...])
    xhat, inv = norm_parts(res)
    hidden = (xhat * gain[...] + shift[...]).astype(BF)
    g_low = cw[...]
    ff = jnp.zeros_like(res)
    gh = jnp.zeros_like(res)
    for j in range(4):
        cols = slice(512 * j, 512 * j + 512)
        pre = nn(hidden, w1[:, cols]) + b1[:, cols]
        half = 0.5 * (1.0 + lax.erf(pre * 0.7071067811865476))
        act = (pre * half).astype(BF)
        ff += nn(act, w2[cols, :])
        slope = half + pre * jnp.exp(-0.5 * pre * pre) * 0.3989422804014327
        gp32 = nt(g_low, w2[cols, :]) * slope
        gp = gp32.astype(BF)
        aw2[:, cols] += tn(g_low, act)
        aw1[:, cols] += tn(hidden, gp)
        gb1[:, cols] += colsum(gp.astype(F32))
        gh += nt(gp, w1[:, cols])
    out = res + (ff + b2[...])
    for i in range(2):
        live = (2 * step + i < cnt[0]).astype(F32)
        low = (out[ROWS * i : ROWS * i + ROWS] * live).astype(BF)
        back = nn(unplace[...], low).astype(BF)
        for r in range(SIDE):
            out_o[i, r] = back[16 * r : 16 * r + SIDE]
    g32 = g_low.astype(F32)
    gb2[...] += colsum(g32)
    gg[...] += colsum(gh * xhat)
    gs[...] += colsum(gh)
    e = gh * gain[...]
    gr = g32 + inv * (
        e - jnp.mean(e, axis=-1, keepdims=True) - xhat * jnp.mean(e * xhat, axis=-1, keepdims=True)
    )
    gr_o[...] = gr
    br = gr.astype(BF)
    gbp[...] += colsum(br.astype(F32))
    awp[...] += tn(att[...], br)
    ga_o[...] = nt(br, wp[...]).astype(BF)

    @pl.when(step == pl.num_programs(0) - 1)
    def _():
        dwp_o[...] = awp[...].astype(BF)
        for j in range(4):
            cols = slice(512 * j, 512 * j + 512)
            dw1_o[j] = aw1[:, cols].astype(BF)
            dw2_o[cols, :] = aw2[:, cols].T.astype(BF)


def back_kernel(
    xw, qkv, pt, ga, gr, unplace, mask, w, gain, shift,
    ig_o, dw_o, gbq, gbv, gg, gs, gbias, aw, gproj,
):
    step = pl.program_id(0)

    @pl.when(step == 0)
    def _():
        for ref in (aw, gbq, gbv, gg, gs, gbias):
            ref[...] = jnp.zeros_like(ref)

    mask_low = mask[...]
    for win in range(4):
        rows = slice(64 * win, 64 * win + 64)
        for g in range(2):
            lo = 256 * g
            db = spread(ga[rows, lo : lo + 256], mask_low)
            qb = spread(qkv[rows, lo : lo + 256], mask_low)
            p_low = pt[0, win, g]
            p = p_low.astype(F32)
            dp = nt(qkv[rows, 2 * D + lo : 2 * D + lo + 256], db)
            ds = (p * (dp - jnp.sum(p * dp, axis=0, keepdims=True))).astype(BF)
            gbias[g] += ds.astype(F32)
            gproj[rows, 2 * D + lo : 2 * D + lo + 256] = nn(p_low, db).astype(BF)
            gproj[rows, D + lo : D + lo + 256] = (nn(ds, qb) * SCALE).astype(BF)
            full = tn(ds, qkv[rows, D + lo : D + lo + 256])
            gproj[rows, lo : lo + 256] = (fold(full, mask_low.astype(F32)) * SCALE).astype(BF)
    gbq[...] += colsum(gproj[:, :D].astype(F32))
    gbv[...] += colsum(gproj[:, 2 * D :].astype(F32))
    xhat, inv = norm_parts(xw[...].astype(F32))
    hidden = (xhat * gain[...] + shift[...]).astype(BF)
    aw[...] += tn(hidden, gproj[...])
    gh = nt(gproj[...], w[...].reshape(D, 3 * D))
    gg[...] += colsum(gh * xhat)
    gs[...] += colsum(gh)
    e = gh * gain[...]
    grad = gr[...] + inv * (
        e - jnp.mean(e, axis=-1, keepdims=True) - xhat * jnp.mean(e * xhat, axis=-1, keepdims=True)
    )
    high = grad.astype(BF)
    low = (grad - high.astype(F32)).astype(BF)
    back = nn(unplace[...], high) + nn(unplace[...], low)
    for r in range(SIDE):
        ig_o[0, r] = back[16 * r : 16 * r + SIDE]

    @pl.when(step == pl.num_programs(0) - 1)
    def _():
        dw_o[...] = aw[...].astype(BF)


def whole(shape):
    return pl.BlockSpec(shape, lambda i: (0,) * len(shape))


def params():
    return pltpu.CompilerParams(
        dimension_semantics=("arbitrary",), vmem_limit_bytes=56 * 1024 * 1024
    )


def sds(shape, dtype):
    return jax.ShapeDtypeStruct(shape, dtype)


def body(
    images, counts, w_qkv, b_qv, w_proj, b_proj, w_fc1, b_fc1, w_fc2, b_fc2,
    norm1_gain, norm1_shift, norm2_gain, norm2_shift, bias_table, cotangent,
):
    n = images.shape[0]
    shards = lax.axis_size("shard")
    me = lax.axis_index("shard")
    vecs = (b_qv, b_proj, b_fc1, b_fc2, norm1_gain, norm1_shift, norm2_gain, norm2_shift)
    sizes = [v.shape[0] for v in vecs]
    reps = lax.axis_size("rep")
    depth = w_qkv.shape[0]
    extra = [jnp.pad(v[None], ((0, 0), (0, 3 * D - v.shape[0]))) for v in vecs]
    extra.append(jnp.zeros((8, 3 * D), BF))
    first = lax.all_gather(jnp.concatenate([w_qkv] + extra, axis=0), "shard", axis=0)
    second = lax.all_gather(
        jnp.concatenate([w_fc1, w_proj], axis=1), "shard", axis=0, tiled=True
    )
    gw_fc2 = lax.all_gather(w_fc2, "shard", axis=0, tiled=True)
    packed = first[:, depth : depth + 8].astype(F32)
    full = [packed[:, i, :size].reshape(1, size * shards) for i, size in enumerate(sizes)]
    bqv, bp, b1, b2, g1, s1, g2, s2 = full

    place = place_matrix()
    place_in = jnp.asarray(place, BF)
    place_out = jnp.asarray(place.T, BF)
    mask = jnp.asarray(head_mask(), BF)
    rel = jnp.asarray(rel_index(), jnp.int32)
    onehot = (jnp.arange(TABLE, dtype=jnp.int32)[:, None] == rel[None, :]).astype(BF)
    bias = lax.dot_general(
        bias_table, onehot, (((0,), (0,)), ((), ())), preferred_element_type=F32
    ).reshape(2, 8, 64, 64).transpose(0, 2, 1, 3)
    bias = (bias[None] + jnp.asarray(penalty_term())).reshape(4, 2, 64, 512)

    smem = pl.BlockSpec(memory_space=pltpu.SMEM)
    image_spec = pl.BlockSpec((1, SIDE, SIDE, D), lambda i: (i, 0, 0, 0))
    rows = lambda count, width: pl.BlockSpec((count, width), lambda i: (i, 0))
    probs_spec = pl.BlockSpec((1, 4, 2, 64, 512), lambda i: (i, 0, 0, 0, 0))
    vec = whole((1, D))
    total = n * ROWS

    xw, cw, qkv, pt, att = pl.pallas_call(
        front_kernel,
        grid=(n,),
        in_specs=[
            smem, image_spec, image_spec, whole((ROWS, 224)), whole((512, 256)),
            whole((4, 2, 64, 512)), whole((shards, depth, 3 * D)), vec, vec, vec, vec,
        ],
        out_specs=[rows(ROWS, D), rows(ROWS, D), rows(ROWS, 3 * D), probs_spec, rows(ROWS, D)],
        out_shape=[
            sds((total, D), BF), sds((total, D), BF), sds((total, 3 * D), BF),
            sds((n, 4, 2, 64, 512), BF), sds((total, D), BF),
        ],
        scratch_shapes=[pltpu.VMEM((224, D), BF)],
        compiler_params=params(),
        cost_estimate=pl.CostEstimate(
            flops=60_000_000_000, bytes_accessed=30_000_000, transcendentals=0
        ),
        name="front",
    )(
        counts, images, cotangent, place_in, mask, bias, first,
        bqv[:, :D], bqv[:, D:], g1, s1,
    )

    wide = whole((1, MLP))
    block_out, gr, ga, dwp, dw1, dw2, gbp, gb1, gb2, gg2, gs2 = pl.pallas_call(
        mlp_kernel,
        grid=(n // 2,),
        in_specs=[
            smem, rows(512, D), rows(512, D), rows(512, D), whole((224, ROWS)),
            pl.BlockSpec((D, D), lambda i: (0, 4)), whole((D, MLP)), whole((MLP, D)),
            vec, wide, vec, vec, vec,
        ],
        out_specs=[
            pl.BlockSpec((2, SIDE, SIDE, D), lambda i: (i, 0, 0, 0)),
            rows(512, D), rows(512, D), whole((D, D)), whole((4, D, D)), whole((MLP, D)),
            vec, wide, vec, vec, vec,
        ],
        out_shape=[
            sds(images.shape, BF), sds((total, D), F32), sds((total, D), BF),
            sds((D, D), BF), sds((4, D, D), BF), sds((MLP, D), BF),
            sds((1, D), F32), sds((1, MLP), F32), sds((1, D), F32), sds((1, D), F32),
            sds((1, D), F32),
        ],
        scratch_shapes=[
            pltpu.VMEM((D, D), F32), pltpu.VMEM((D, MLP), F32), pltpu.VMEM((D, MLP), F32),
        ],
        compiler_params=params(),
        cost_estimate=pl.CostEstimate(
            flops=60_000_000_000, bytes_accessed=30_000_000, transcendentals=0
        ),
        name="mlp",
    )(counts, xw, cw, att, place_out, second, second, gw_fc2, bp, b1, b2, g2, s2)

    both = ("rep", "shard")
    deep = D // (shards * reps)
    split = lambda term: term.reshape(shards, reps, -1, term.shape[-1]).swapaxes(0, 1)
    cut = dw1.reshape(4, shards, reps, deep, D).transpose(2, 1, 0, 3, 4)
    joined = jnp.concatenate(
        [split(dw2), split(dwp), cut.reshape(reps, shards, 4 * deep, D)], axis=2
    ).reshape(-1, D)
    part_mlp = lax.psum_scatter(joined, both, scatter_dimension=0, tiled=True)
    own_mlp = lax.all_gather(part_mlp, "rep", axis=0)
    own_two = own_mlp[:, : 4 * deep].reshape(-1, D)
    own_proj = own_mlp[:, 4 * deep : 5 * deep].reshape(-1, D)
    own_one = own_mlp[:, 5 * deep :].reshape(reps, 4, deep, D).swapaxes(1, 2).reshape(-1, MLP)

    image_grad, dwq, gbq, gbv, gg1, gs1, gbias = pl.pallas_call(
        back_kernel,
        grid=(n,),
        in_specs=[
            rows(ROWS, D), rows(ROWS, 3 * D), probs_spec, rows(ROWS, D), rows(ROWS, D),
            whole((224, ROWS)), whole((512, 256)), whole((shards, depth, 3 * D)), vec, vec,
        ],
        out_specs=[
            image_spec, whole((D, 3 * D)), vec, vec, vec, vec, whole((2, 64, 512)),
        ],
        out_shape=[
            sds(images.shape, F32), sds((D, 3 * D), BF), sds((1, D), F32), sds((1, D), F32),
            sds((1, D), F32), sds((1, D), F32), sds((2, 64, 512), F32),
        ],
        scratch_shapes=[pltpu.VMEM((D, 3 * D), F32), pltpu.VMEM((ROWS, 3 * D), BF)],
        compiler_params=params(),
        cost_estimate=pl.CostEstimate(
            flops=80_000_000_000, bytes_accessed=30_000_000, transcendentals=0
        ),
        name="back",
    )(xw, qkv, pt, ga, gr, place_out, mask, first, g1, s1)

    part_qkv = lax.psum_scatter(
        split(dwq).reshape(-1, 3 * D), both, scatter_dimension=0, tiled=True
    )
    own_qkv = lax.all_gather(part_qkv, "rep", axis=0, tiled=True)
    own = [term.astype(F32) for term in (own_qkv, own_proj, own_one, own_two)]
    by_head = gbias.reshape(2, 64, 8, 64).transpose(0, 2, 1, 3).reshape(HEADS, 4096)
    table = lax.dot_general(
        onehot.astype(F32), by_head, (((1,), (1,)), ((), ())),
        precision=lax.Precision.HIGHEST, preferred_element_type=F32,
    )
    terms = (jnp.concatenate([gbq, gbv], axis=1), gbp, gb1, gb2, gg1, gs1, gg2, gs2)
    flat = jnp.concatenate([t.reshape(-1) for t in terms] + [table.reshape(-1)])
    flat = lax.psum(flat, ("rep", "shard"))
    small, at = [], 0
    for size in sizes:
        small.append(lax.dynamic_slice_in_dim(flat, at + me * size, size))
        at += size * shards
    table = flat[at:].reshape(TABLE, HEADS)
    return (
        block_out, image_grad, own[0], small[0], own[1], small[1], own[2], small[2],
        own[3], small[3], small[4], small[5], small[6], small[7], table,
    )


def solution(mesh):
    img = P(("rep", "shard"), None, None, None)
    row, vec = P("shard", None), P("shard")
    weights = (row, vec, row, vec, row, vec, row, vec, vec, vec, vec, vec)
    return jax.shard_map(
        body,
        mesh=mesh,
        in_specs=(img, P(("rep", "shard"))) + weights + (P(), img),
        out_specs=(img, img) + weights + (P(),),
        check_vma=False,
    )
```
